32 devices in a mesh: groups: 2 (over x), gx: 16 (over z, y, core).
Axes of the slice: x: 2, y: 2, z: 4, core: 2. Of those that a mesh axis runs over, the one named last changes fastest.
Arguments:
- fine_in: float32 [48, 64, 16, 32], P(None, ('groups', 'gx')), parts along dimension 1, may hold values from -6 to 6
- coarse_in: float32 [96, 32, 8, 16], P(None, ('groups', 'gx')), parts along dimension 1, may hold values from -6 to 6
- fine_wa: float32 [48, 48, 3, 3, 3], replicated, may hold values from -0.15625 to 0.15625
- fine_ba: float32 [48], replicated, may hold values from -3 to 3
- fine_wb: float32 [48, 48, 3, 3, 3], replicated, may hold values from -0.15625 to 0.15625
- fine_bb: float32 [48], replicated, may hold values from -3 to 3
- coarse_wa: float32 [96, 96, 3, 3, 3], replicated, may hold values from -0.125 to 0.125
- coarse_ba: float32 [96], replicated, may hold values from -3 to 3
- coarse_wb: float32 [96, 96, 3, 3, 3], replicated, may hold values from -0.125 to 0.125
- coarse_bb: float32 [96], replicated, may hold values from -3 to 3
- down_w: float32 [96, 48, 3, 3, 3], replicated, may hold values from -0.15625 to 0.15625
- down_b: float32 [96], replicated, may hold values from -3 to 3
- up_w: float32 [48, 96], replicated, may hold values from -0.625 to 0.625
- up_b: float32 [48], replicated, may hold values from -3 to 3
Outputs:
- fine_out: float32 [48, 64, 16, 32], P(None, ('groups', 'gx')), parts along dimension 1
- coarse_out: float32 [96, 32, 8, 16], P(None, ('groups', 'gx')), parts along dimension 1
The draws below stay inside these ranges and needn't reach their ends.
There are 2 independent parts, one for each index of `groups`. The reference program is written for one: setup_inputs(seed, part) draws one part's arguments, and reference() takes and returns one part's arrays. A program takes and returns all parts, laid end to end along the dimension named above; an argument that names none is the same for every part. Nothing has to cross between parts.
All inputs are finite; a program needn't handle non-finite values.
Results may differ from the reference program's by a relative error of at most 0.000058.
Values sent between devices are 32-bit elements; how exact they have to be, the bound alone decides.
A program may use at most 128 MiB of HBM per device.

```python
import jax
import jax.numpy as jnp
from jax import lax

CF = 48
CC = 96
DEPTH = 16
X = 32
Y = 32
XC = 16
YC = 16
DC = 8


def block_levels(own_key, extent, split, least, largest):
    def one(dim, shards_of):
        steps = jax.random.uniform(jax.random.fold_in(jax.random.fold_in(own_key, 6), dim), (shards_of,), jnp.float32, least / len(split), largest / len(split))
        return jnp.repeat(jnp.exp(steps), extent[dim] // shards_of).reshape((-1,) + (1,) * (len(extent) - dim - 1))

    factor_of = one(*split[0])
    for cut in split[1:]:
        factor_of = factor_of * one(*cut)
    return factor_of


def normal_values(own_key, shape, width, most, shards=(), kind=jnp.bfloat16):
    factor_of = block_levels(own_key, shape, shards, -0.22, 0.18) if shards else 1.0
    array = jax.random.normal(own_key, shape, jnp.float32) * width * factor_of
    return jnp.minimum(jnp.maximum(array, -most), most).astype(kind)


def setup_inputs(seed: int = 0, part: int = 0) -> dict:
    key_of = jax.random.split(jax.random.key(seed), 15)
    part_splits = jax.random.split(jax.random.fold_in(key_of[14], part), 15)
    return {
        "fine_in": normal_values(part_splits[0], (CF, X, DEPTH, Y), 1.0, 6.0, ((1, 16),), jnp.float32),
        "coarse_in": normal_values(part_splits[1], (CC, YC, DC, XC), 1.0, 6.0, ((1, 16),), jnp.float32),
        "fine_wa": normal_values(key_of[2], (CF, CF, 3, 3, 3), (27 * CF) ** -0.5, 0.15625, (), jnp.float32),
        "fine_ba": normal_values(key_of[3], (CF,), 0.5, 3.0, (), jnp.float32),
        "fine_wb": normal_values(key_of[4], (CF, CF, 3, 3, 3), (27 * CF) ** -0.5, 0.15625, (), jnp.float32),
        "fine_bb": normal_values(key_of[5], (CF,), 0.5, 3.0, (), jnp.float32),
        "coarse_wa": normal_values(key_of[6], (CC, CC, 3, 3, 3), (27 * CC) ** -0.5, 0.125, (), jnp.float32),
        "coarse_ba": normal_values(key_of[7], (CC,), 0.5, 3.0, (), jnp.float32),
        "coarse_wb": normal_values(key_of[8], (CC, CC, 3, 3, 3), (27 * CC) ** -0.5, 0.125, (), jnp.float32),
        "coarse_bb": normal_values(key_of[9], (CC,), 0.5, 3.0, (), jnp.float32),
        "down_w": normal_values(key_of[10], (CC, CF, 3, 3, 3), (27 * CF) ** -0.5, 0.15625, (), jnp.float32),
        "down_b": normal_values(key_of[11], (CC,), 0.5, 3.0, (), jnp.float32),
        "up_w": normal_values(key_of[12], (CF, CC), CC ** -0.5, 0.625, (), jnp.float32),
        "up_b": normal_values(key_of[13], (CF,), 0.5, 3.0, (), jnp.float32),
    }


def convolve(padded, weights, stride):
    return lax.conv_general_dilated(padded[None], weights, (stride, stride, stride), "VALID", dimension_numbers=("NCHWD", "OIHWD", "NCHWD"), precision=lax.Precision.HIGHEST)[0]


def pad_cells(field):
    return jnp.pad(field, ((0, 0), (1, 1), (1, 1), (1, 1)))


def residual_block(field, wa, ba, wb, bb):
    middle = jax.nn.relu(convolve(pad_cells(field), wa, 1) + ba[:, None, None, None])
    return jax.nn.relu(field + convolve(pad_cells(middle), wb, 1) + bb[:, None, None, None])


def reference(fine_in, coarse_in, fine_wa, fine_ba, fine_wb, fine_bb, coarse_wa, coarse_ba, coarse_wb, coarse_bb, down_w, down_b, up_w, up_b):
    fine = residual_block(fine_in, fine_wa, fine_ba, fine_wb, fine_bb)
    coarse = residual_block(coarse_in, coarse_wa, coarse_ba, coarse_wb, coarse_bb)
    reduced = convolve(pad_cells(fine), down_w, 2) + down_b[:, None, None, None]
    reduced = jnp.transpose(reduced, (0, 3, 2, 1))
    coarse_out = jax.nn.gelu(coarse + reduced, approximate=False)
    projected = jnp.einsum("oc,cydx->oydx", up_w, coarse, precision=lax.Precision.HIGHEST) + up_b[:, None, None, None]
    projected = jnp.transpose(projected, (0, 3, 2, 1))
    raised = jnp.repeat(jnp.repeat(jnp.repeat(projected, 2, axis=1), 2, axis=2), 2, axis=3)
    fine_out = jax.nn.gelu(fine + raised, approximate=False)
    return fine_out, coarse_out
```

```python
import functools

import jax
import jax.numpy as jnp
from jax import lax
from jax.experimental import pallas as pl
from jax.experimental.pallas import tpu as pltpu
from jax.sharding import PartitionSpec as P

ROWS = 512


def halves(value):
    high = value.astype(jnp.bfloat16)
    return high, (value - high.astype(jnp.float32)).astype(jnp.bfloat16)


def put_patches(value, high_ref, low_ref, slot, width, base=None):
    rows, channels = value.shape
    place = lax.rem(lax.broadcasted_iota(jnp.int32, (rows, channels), 0), width)
    before = jnp.where(place == 0, 0.0, pltpu.roll(value, 1, 0))
    after = jnp.where(place == width - 1, 0.0, pltpu.roll(value, rows - 1, 0))
    for k, part in enumerate((before, value, after)):
        high, low = halves(part)
        at = pl.ds(k * channels, channels)
        high_ref[slot, pl.ds(width, rows), at] = high
        low_ref[slot, pl.ds(width, rows), at] = low


def clear_rims(high_ref, low_ref, width):
    slots, rows, lanes = high_ref.shape
    zero = jnp.zeros((slots, width, lanes), jnp.bfloat16)
    for ref in (high_ref, low_ref):
        ref[:, pl.ds(0, width), :] = zero
        ref[:, pl.ds(rows - width, width), :] = zero


def product(high, low, weights):
    out = weights.shape[1] // 2
    both = jnp.dot(high, weights, preferred_element_type=jnp.float32)
    third = jnp.dot(low, weights[:, :out], preferred_element_type=jnp.float32)
    return both[:, :out] + both[:, out:] + third


def conv_chunk(high_ref, low_ref, w_ref, slot, start, rows, width):
    total = None
    for p in range(3):
        for q in range(3):
            at = pl.ds(pl.multiple_of(start + q * width, 16), rows)
            term = product(high_ref[slot + p, at, :], low_ref[slot + p, at, :], w_ref[3 * p + q])
            total = term if total is None else total + term
    return total


def conv_plane(high_ref, low_ref, w_ref, temp_ref, slot, width, finish):
    rows = temp_ref.shape[0]
    step = min(ROWS, rows)

    def body(i, _):
        start = i * step
        at = pl.ds(pl.multiple_of(start, 16), step)
        temp_ref[at, :] = finish(
            conv_chunk(high_ref, low_ref, w_ref, slot, start, step, width), at
        )
        return 0

    if rows == step:
        temp_ref[...] = finish(
            conv_chunk(high_ref, low_ref, w_ref, slot, 0, step, width), pl.ds(0, step)
        )
    else:
        lax.fori_loop(0, rows // step, body, 0)


def compute(
    count, width, narrow,
    f7, c5, wfa, bfa, wfb, bfb, wca, bca, wcb, bcb, wd, bd, wu, bu,
    fine_ref, coarse_ref, moved_ref, projected_ref,
    fhi, flo, chi, clo, ftemp, ctemp, mtemp, *staged,
):
    me = lax.axis_index("gx")

    def plane_of(j):
        if not staged:
            return f7.at[j]
        copy = pltpu.make_async_copy(f7.at[j], staged[0], staged[1])
        copy.start()
        copy.wait()
        return staged[0]

    clear_rims(chi, clo, narrow)

    def coarse_load(j, _):
        put_patches(c5[j], chi, clo, j, narrow)
        return 0

    lax.fori_loop(0, 5, coarse_load, 0)

    def coarse_mid(j, _):
        y = me - 1 + j
        inside = jnp.where((y >= 0) & (y < count), 1.0, 0.0)
        conv_plane(
            chi, clo, wca, ctemp, j, narrow,
            lambda total, at: jnp.maximum(total + bca[...], 0.0) * inside,
        )
        put_patches(ctemp[...], chi, clo, j, narrow)
        return 0

    lax.fori_loop(0, 3, coarse_mid, 0)
    conv_plane(
        chi, clo, wcb, ctemp, 0, narrow,
        lambda total, at: jnp.maximum(c5[2, at, :] + total + bcb[...], 0.0),
    )
    coarse = ctemp[...]
    coarse_ref[...] = coarse
    projected_ref[...] = product(*halves(coarse), wu[...]) + bu[...]

    clear_rims(fhi, flo, width)

    def fine_load(j, _):
        put_patches(plane_of(j)[...], fhi, flo, j, width)
        return 0

    lax.fori_loop(0, 7, fine_load, 0)

    def fine_mid(j, _):
        x = 2 * me - 2 + j
        inside = jnp.where((x >= 0) & (x < 2 * count), 1.0, 0.0)
        conv_plane(
            fhi, flo, wfa, ftemp, j, width,
            lambda total, at: jnp.maximum(total + bfa[...], 0.0) * inside,
        )
        put_patches(ftemp[...], fhi, flo, j, width)
        return 0

    lax.fori_loop(0, 5, fine_mid, 0)

    def fine_last(j, _):
        x = 2 * me - 1 + j
        inside = jnp.where(x >= 0, 1.0, 0.0)
        own = plane_of(j + 2)
        conv_plane(
            fhi, flo, wfb, ftemp, j, width,
            lambda total, at: jnp.maximum(own[at, :] + total + bfb[...], 0.0) * inside,
        )
        fine = ftemp[...]
        put_patches(fine, fhi, flo, j, width)
        fine_ref[jnp.maximum(j - 1, 0)] = fine
        return 0

    lax.fori_loop(0, 3, fine_last, 0)

    levels = moved_ref.shape[0] // narrow
    some = max(1, min(levels, ROWS // width))
    for first in range(0, levels, some):
        total = None
        for p in range(3):
            for q in range(3):
                def rows_of(ref):
                    return jnp.concatenate(
                        [ref[p, pl.ds((2 * b + q) * width, width), :] for b in range(first, first + some)],
                        axis=0,
                    )
                term = product(rows_of(fhi), rows_of(flo), wd[3 * p + q])
                total = term if total is None else total + term
        channels = total.shape[1]
        mtemp[:, pl.ds(0, channels)] = total + bd[...]
        moved_ref[pl.ds(first * narrow, some * narrow), :] = mtemp[
            pl.ds(0, some * narrow, stride=2), :
        ][:, :channels]


def split_weights(w):
    out, inner = w.shape[:2]
    moved = jnp.transpose(w, (2, 3, 4, 1, 0)).reshape(9, 3 * inner, out)
    high = lax.reduce_precision(moved, 8, 7)
    return jnp.concatenate([high, moved - high], axis=2).astype(jnp.bfloat16)


def shifted(value, steps):
    count = lax.axis_size("gx")
    pairs = [(i, i + steps) for i in range(count) if 0 <= i + steps < count]
    return lax.ppermute(value, "gx", pairs)


def per_device(
    fine_in, coarse_in,
    fine_wa, fine_ba, fine_wb, fine_bb,
    coarse_wa, coarse_ba, coarse_wb, coarse_bb,
    down_w, down_b, up_w, up_b,
):
    count = lax.axis_size("gx")
    cf, planes, depth, width = fine_in.shape
    cc, _, levels, narrow = coarse_in.shape
    own = jnp.transpose(fine_in, (1, 2, 3, 0)).reshape(planes, depth * width, cf)
    slab = jnp.transpose(coarse_in, (1, 2, 3, 0)).reshape(1, levels * narrow, cc)
    f7 = jnp.concatenate(
        [shifted(own[1:], 2), shifted(own, 1), own, shifted(own, -1)], axis=0
    )
    c5 = jnp.concatenate(
        [shifted(slab, 2), shifted(slab, 1), slab, shifted(slab, -1), shifted(slab, -2)], axis=0
    )
    up = up_w.T
    up_high = lax.reduce_precision(up, 8, 7)
    wu = jnp.concatenate([up_high, up - up_high], axis=1).astype(jnp.bfloat16)
    frows, crows = depth * width, levels * narrow
    some = max(1, min(levels, ROWS // width))
    vmem = pl.BlockSpec(memory_space=pltpu.VMEM)
    large = frows > 1024
    stage = [pltpu.VMEM((frows, cf), jnp.float32), pltpu.SemaphoreType.DMA] if large else []
    fine, coarse, moved, projected = pl.pallas_call(
        functools.partial(compute, count, width, narrow),
        out_shape=(
            jax.ShapeDtypeStruct((planes, frows, cf), jnp.float32),
            jax.ShapeDtypeStruct((crows, cc), jnp.float32),
            jax.ShapeDtypeStruct((crows, cc), jnp.float32),
            jax.ShapeDtypeStruct((crows, cf), jnp.float32),
        ),
        in_specs=[pl.BlockSpec(memory_space=pl.ANY) if large else vmem] + [vmem] * 13,
        out_specs=(vmem,) * 4,
        scratch_shapes=[
            pltpu.VMEM((7, frows + 2 * width, 3 * cf), jnp.bfloat16),
            pltpu.VMEM((7, frows + 2 * width, 3 * cf), jnp.bfloat16),
            pltpu.VMEM((5, crows + 2 * narrow, 3 * cc), jnp.bfloat16),
            pltpu.VMEM((5, crows + 2 * narrow, 3 * cc), jnp.bfloat16),
            pltpu.VMEM((frows, cf), jnp.float32),
            pltpu.VMEM((crows, cc), jnp.float32),
            pltpu.VMEM((some * width, 128), jnp.float32),
        ] + stage,
        compiler_params=pltpu.CompilerParams(vmem_limit_bytes=(60 if large else 30) * 2**20),
        cost_estimate=pl.CostEstimate(flops=10**9, bytes_accessed=6 * 10**6, transcendentals=0),
    )(
        f7, c5,
        split_weights(fine_wa), fine_ba[None], split_weights(fine_wb), fine_bb[None],
        split_weights(coarse_wa), coarse_ba[None], split_weights(coarse_wb), coarse_bb[None],
        split_weights(down_w), down_b[None], wu, up_b[None],
    )
    both = jnp.concatenate(
        [
            jnp.transpose(moved.reshape(levels, narrow, cc), (1, 0, 2)),
            jnp.transpose(projected.reshape(levels, narrow, cf), (1, 0, 2)),
        ],
        axis=2,
    )
    arrived = lax.all_to_all(both, "gx", split_axis=0, concat_axis=0, tiled=True)
    reduced = jnp.transpose(arrived[:, :, :cc], (1, 0, 2))
    raised = jnp.transpose(arrived[:, :, cc:], (1, 0, 2))
    coarse_out = jax.nn.gelu(coarse.reshape(levels, narrow, cc) + reduced, approximate=False)
    raised = jnp.broadcast_to(
        raised[None, :, None, :, None, :], (planes, levels, depth // levels, narrow, width // narrow, cf)
    ).reshape(planes, depth, width, cf)
    fine_out = jax.nn.gelu(fine.reshape(planes, depth, width, cf) + raised, approximate=False)
    return (
        jnp.transpose(fine_out, (3, 0, 1, 2)),
        jnp.transpose(coarse_out, (2, 0, 1))[:, None],
    )


def solution(mesh):
    split = P(None, ("groups", "gx"), None, None)
    return jax.shard_map(
        per_device,
        mesh=mesh,
        in_specs=(split, split) + (P(),) * 12,
        out_specs=(split, split),
        check_vma=False,
    )
```

```python
import functools

import jax
import jax.numpy as jnp
from jax import lax
from jax.experimental import pallas as pl
from jax.experimental.pallas import tpu as pltpu
from jax.sharding import PartitionSpec as P

ROWS = 512


def halves(value):
    high = value.astype(jnp.bfloat16)
    return high, (value - high.astype(jnp.float32)).astype(jnp.bfloat16)


def put_patches(value, high_ref, low_ref, slot, width, base=None):
    rows, channels = value.shape
    place = lax.rem(lax.broadcasted_iota(jnp.int32, (rows, channels), 0), width)
    before = jnp.where(place == 0, 0.0, pltpu.roll(value, 1, 0))
    after = jnp.where(place == width - 1, 0.0, pltpu.roll(value, rows - 1, 0))
    for k, part in enumerate((before, value, after)):
        high, low = halves(part)
        at = pl.ds(k * channels, channels)
        high_ref[slot, pl.ds(width, rows), at] = high
        low_ref[slot, pl.ds(width, rows), at] = low


def clear_rims(high_ref, low_ref, width):
    slots, rows, lanes = high_ref.shape
    zero = jnp.zeros((slots, width, lanes), jnp.bfloat16)
    for ref in (high_ref, low_ref):
        ref[:, pl.ds(0, width), :] = zero
        ref[:, pl.ds(rows - width, width), :] = zero


def product(high, low, weights):
    out = weights.shape[1] // 2
    both = jnp.dot(high, weights, preferred_element_type=jnp.float32)
    third = jnp.dot(low, weights[:, :out], preferred_element_type=jnp.float32)
    return both[:, :out] + both[:, out:] + third


def conv_chunk(high_ref, low_ref, w_ref, slot, start, rows, width):
    total = None
    for p in range(3):
        for q in range(3):
            at = pl.ds(pl.multiple_of(start + q * width, 16), rows)
            term = product(high_ref[slot + p, at, :], low_ref[slot + p, at, :], w_ref[3 * p + q])
            total = term if total is None else total + term
    return total


def conv_plane(high_ref, low_ref, w_ref, temp_ref, slot, width, finish):
    rows = temp_ref.shape[0]
    step = min(ROWS, rows)

    def body(i, _):
        start = i * step
        at = pl.ds(pl.multiple_of(start, 16), step)
        temp_ref[at, :] = finish(
            conv_chunk(high_ref, low_ref, w_ref, slot, start, step, width), at
        )
        return 0

    if rows == step:
        temp_ref[...] = finish(
            conv_chunk(high_ref, low_ref, w_ref, slot, 0, step, width), pl.ds(0, step)
        )
    else:
        lax.fori_loop(0, rows // step, body, 0)


def compute(
    count, width, narrow,
    f7, c5, wfa, bfa, wfb, bfb, wca, bca, wcb, bcb, wd, bd, wu, bu,
    fine_ref, coarse_ref, moved_ref, projected_ref,
    fhi, flo, chi, clo, ftemp, ctemp, mtemp, *staged,
):
    me = lax.axis_index("gx")

    def plane_of(j):
        if not staged:
            return f7.at[j]
        copy = pltpu.make_async_copy(f7.at[j], staged[0], staged[1])
        copy.start()
        copy.wait()
        return staged[0]

    clear_rims(chi, clo, narrow)

    def coarse_load(j, _):
        put_patches(c5[j], chi, clo, j, narrow)
        return 0

    lax.fori_loop(0, 5, coarse_load, 0)

    def coarse_mid(j, _):
        y = me - 1 + j
        inside = jnp.where((y >= 0) & (y < count), 1.0, 0.0)
        conv_plane(
            chi, clo, wca, ctemp, j, narrow,
            lambda total, at: jnp.maximum(total + bca[...], 0.0) * inside,
        )
        put_patches(ctemp[...], chi, clo, j, narrow)
        return 0

    lax.fori_loop(0, 3, coarse_mid, 0)
    conv_plane(
        chi, clo, wcb, ctemp, 0, narrow,
        lambda total, at: jnp.maximum(c5[2, at, :] + total + bcb[...], 0.0),
    )
    coarse = ctemp[...]
    coarse_ref[...] = coarse
    projected_ref[...] = product(*halves(coarse), wu[...]) + bu[...]

    clear_rims(fhi, flo, width)

    def fine_load(j, _):
        put_patches(plane_of(j)[...], fhi, flo, j, width)
        return 0

    lax.fori_loop(0, 7, fine_load, 0)

    def fine_mid(j, _):
        x = 2 * me - 2 + j
        inside = jnp.where((x >= 0) & (x < 2 * count), 1.0, 0.0)
        conv_plane(
            fhi, flo, wfa, ftemp, j, width,
            lambda total, at: jnp.maximum(total + bfa[...], 0.0) * inside,
        )
        put_patches(ftemp[...], fhi, flo, j, width)
        return 0

    lax.fori_loop(0, 5, fine_mid, 0)

    def fine_last(j, _):
        x = 2 * me - 1 + j
        inside = jnp.where(x >= 0, 1.0, 0.0)
        own = plane_of(j + 2)
        conv_plane(
            fhi, flo, wfb, ftemp, j, width,
            lambda total, at: jnp.maximum(own[at, :] + total + bfb[...], 0.0) * inside,
        )
        fine = ftemp[...]
        put_patches(fine, fhi, flo, j, width)
        fine_ref[jnp.maximum(j - 1, 0)] = fine
        return 0

    lax.fori_loop(0, 3, fine_last, 0)

    levels = moved_ref.shape[0] // narrow
    some = max(1, min(levels, ROWS // width))
    for first in range(0, levels, some):
        total = None
        for p in range(3):
            for q in range(3):
                def rows_of(ref):
                    return jnp.concatenate(
                        [ref[p, pl.ds((2 * b + q) * width, width), :] for b in range(first, first + some)],
                        axis=0,
                    )
                term = product(rows_of(fhi), rows_of(flo), wd[3 * p + q])
                total = term if total is None else total + term
        channels = total.shape[1]
        mtemp[:, pl.ds(0, channels)] = total + bd[...]
        moved_ref[pl.ds(first * narrow, some * narrow), :] = mtemp[
            pl.ds(0, some * narrow, stride=2), :
        ][:, :channels]


def prepare(raw_ref, out_ref, transposed):
    def body(t, _):
        for r in range(3):
            w = raw_ref[3 * t + r]
            if transposed:
                w = w.T
            high, low = halves(w)
            inner, out = w.shape
            out_ref[t, pl.ds(r * inner, inner), pl.ds(0, out)] = high
            out_ref[t, pl.ds(r * inner, inner), pl.ds(out, out)] = low
        return 0

    lax.fori_loop(0, 9, body, 0)


def joined(
    count, width, narrow,
    own, slab, rfa, bfa, rfb, bfb, rca, bca, rcb, bcb, rd, bd, up, bu,
    fine_ref, coarse_ref,
    fhi, flo, chi, clo, ftemp, ctemp, mtemp,
    wfa, wfb, wca, wcb, wd,
    pair_send, half_send, pair_low, pair_high, half_low, crecv,
    psend, precv, msend, mrecv, spread,
    hs, hr, ps, pr, ms, mr,
):
    me = lax.axis_index("gx")
    mesh_id = pl.DeviceIdType.MESH
    rows, cf = ftemp.shape
    cc = ctemp.shape[1]
    levels = ctemp.shape[0] // narrow
    half = rows // 2
    barrier = pltpu.get_barrier_semaphore()

    def greet(k, _):
        pl.semaphore_signal(
            barrier, inc=1, device_id={"gx": lax.rem(me + k, count)}, device_id_type=mesh_id
        )
        return 0

    lax.fori_loop(1, count, greet, 0)

    pair_send[:, pl.ds(0, cf)] = own[0]
    pair_send[:, pl.ds(cf, cf)] = own[1]
    half_send[:, pl.ds(0, cf)] = own[1, pl.ds(0, half), :]
    half_send[:, pl.ds(cf, cf)] = own[1, pl.ds(half, half), :]
    pl.semaphore_wait(barrier, count - 1)

    halos = (
        (slab.at[0], crecv.at[1], 1),
        (slab.at[0], crecv.at[2], -1),
        (slab.at[0], crecv.at[0], 2),
        (slab.at[0], crecv.at[3], -2),
        (pair_send, pair_low, 1),
        (pair_send, pair_high, -1),
        (half_send, half_low, 2),
    )

    def copy_of(k):
        source, target, step = halos[k]
        return pltpu.make_async_remote_copy(
            src_ref=source, dst_ref=target, send_sem=hs.at[k], recv_sem=hr.at[k],
            device_id={"gx": lax.rem(me + step + count, count)}, device_id_type=mesh_id,
        )

    def sends(k):
        step = halos[k][2]
        return (me + step >= 0) & (me + step < count)

    def receives(k):
        step = halos[k][2]
        return (me - step >= 0) & (me - step < count)

    for k in range(7):
        @pl.when(sends(k))
        def _():
            copy_of(k).start()

        @pl.when(jnp.logical_not(receives(k)))
        def _():
            target = halos[k][1]
            target[...] = jnp.zeros(target.shape, jnp.float32)

    prepare(rca, wca, True)
    prepare(rcb, wcb, True)
    clear_rims(chi, clo, narrow)
    clear_rims(fhi, flo, width)
    put_patches(slab[0], chi, clo, 2, narrow)

    def landed(k):
        @pl.when(receives(k))
        def _():
            copy_of(k).wait_recv()

    for k in range(4):
        landed(k)
    for k, slot in enumerate((0, 1, 3, 4)):
        put_patches(crecv[k], chi, clo, slot, narrow)

    def coarse_mid(j, _):
        y = me - 1 + j
        inside = jnp.where((y >= 0) & (y < count), 1.0, 0.0)
        conv_plane(
            chi, clo, wca, ctemp, j, narrow,
            lambda total, at: jnp.maximum(total + bca[...], 0.0) * inside,
        )
        put_patches(ctemp[...], chi, clo, j, narrow)
        return 0

    lax.fori_loop(0, 3, coarse_mid, 0)
    conv_plane(
        chi, clo, wcb, ctemp, 0, narrow,
        lambda total, at: jnp.maximum(slab[0, at, :] + total + bcb[...], 0.0),
    )
    uh, ul = halves(up[...].T)
    projected = product(*halves(ctemp[...]), jnp.concatenate([uh, ul], axis=1)) + bu[...]
    for d in range(levels):
        psend[:, d, :] = projected[d * narrow : (d + 1) * narrow]

    def exchange(send, recv, send_sem, recv_sem, k):
        target = lax.rem(me + k, count)
        return pltpu.make_async_remote_copy(
            src_ref=send.at[target], dst_ref=recv.at[me],
            send_sem=send_sem.at[k], recv_sem=recv_sem.at[k],
            device_id={"gx": target}, device_id_type=mesh_id,
        )

    def start_all(send, recv, send_sem, recv_sem):
        def body(k, _):
            exchange(send, recv, send_sem, recv_sem, k).start()
            return 0

        lax.fori_loop(1, count, body, 0)
        recv[me] = send[me]

    def wait_all(send, recv, send_sem, recv_sem):
        def body(k, _):
            source = lax.rem(me - k + count, count)
            pltpu.make_async_remote_copy(
                src_ref=send.at[source], dst_ref=recv.at[source],
                send_sem=send_sem.at[k], recv_sem=recv_sem.at[k],
                device_id={"gx": source}, device_id_type=mesh_id,
            ).wait_recv()
            exchange(send, recv, send_sem, recv_sem, k).wait_send()
            return 0

        lax.fori_loop(1, count, body, 0)

    start_all(psend, precv, ps, pr)

    prepare(rfa, wfa, True)
    put_patches(own[0], fhi, flo, 3, width)
    put_patches(own[1], fhi, flo, 4, width)
    for k in range(4, 7):
        landed(k)
    put_patches(
        jnp.concatenate([half_low[:, pl.ds(0, cf)], half_low[:, pl.ds(cf, cf)]], axis=0),
        fhi, flo, 0, width,
    )
    put_patches(pair_low[:, pl.ds(0, cf)], fhi, flo, 1, width)
    put_patches(pair_low[:, pl.ds(cf, cf)], fhi, flo, 2, width)
    put_patches(pair_high[:, pl.ds(0, cf)], fhi, flo, 5, width)
    put_patches(pair_high[:, pl.ds(cf, cf)], fhi, flo, 6, width)

    def fine_mid(j, _):
        x = 2 * me - 2 + j
        inside = jnp.where((x >= 0) & (x < 2 * count), 1.0, 0.0)
        conv_plane(
            fhi, flo, wfa, ftemp, j, width,
            lambda total, at: jnp.maximum(total + bfa[...], 0.0) * inside,
        )
        put_patches(ftemp[...], fhi, flo, j, width)
        return 0

    lax.fori_loop(0, 5, fine_mid, 0)
    prepare(rfb, wfb, True)
    prepare(rd, wd, False)
    before = jnp.where(me > 0, 1.0, 0.0)
    conv_plane(
        fhi, flo, wfb, ftemp, 0, width,
        lambda total, at: jnp.maximum(pair_low[at, pl.ds(cf, cf)] + total + bfb[...], 0.0) * before,
    )
    put_patches(ftemp[...], fhi, flo, 0, width)

    def fine_last(j, _):
        conv_plane(
            fhi, flo, wfb, ftemp, j, width,
            lambda total, at: jnp.maximum(own[j - 1, at, :] + total + bfb[...], 0.0),
        )
        put_patches(ftemp[...], fhi, flo, j, width)
        fine_ref[j - 1] = ftemp[...]
        return 0

    lax.fori_loop(1, 3, fine_last, 0)

    total = None
    for p in range(3):
        for q in range(3):
            def rows_of(ref):
                return jnp.concatenate(
                    [ref[p, pl.ds((2 * b + q) * width, width), :] for b in range(levels)], axis=0
                )
            term = product(rows_of(fhi), rows_of(flo), wd[3 * p + q])
            total = term if total is None else total + term
    mtemp[:, pl.ds(0, cc)] = total + bd[...]
    for b in range(levels):
        msend[:, b, :] = mtemp[pl.ds(b * width, narrow, stride=2), :][:, :cc]
    start_all(msend, mrecv, ms, mr)

    wait_all(psend, precv, ps, pr)
    for d in range(rows // width):
        block = precv[:, d // 2, :]
        for s in range(2):
            spread[pl.ds(d * width + s, narrow, stride=2), pl.ds(0, cf)] = block
    for x in range(2):
        fine_ref[x] = fine_ref[x] + spread[:, pl.ds(0, cf)]
    for k in range(7):
        @pl.when(sends(k))
        def _():
            copy_of(k).wait_send()

    wait_all(msend, mrecv, ms, mr)
    for d in range(levels):
        at = pl.ds(d * narrow, narrow)
        coarse_ref[at, :] = ctemp[at, :] + mrecv[:, d, :]


def joined_call(count, width, narrow, own, slab, operands):
    planes, rows, cf = own.shape
    _, crows, cc = slab.shape
    levels = crows // narrow
    f32, bf16 = jnp.float32, jnp.bfloat16
    vmem = pl.BlockSpec(memory_space=pltpu.VMEM)
    dma = pltpu.SemaphoreType.DMA
    return pl.pallas_call(
        functools.partial(joined, count, width, narrow),
        out_shape=(
            jax.ShapeDtypeStruct((planes, rows, cf), f32),
            jax.ShapeDtypeStruct((crows, cc), f32),
        ),
        in_specs=[vmem] * 14,
        out_specs=(vmem,) * 2,
        scratch_shapes=[
            pltpu.VMEM((7, rows + 2 * width, 3 * cf), bf16),
            pltpu.VMEM((7, rows + 2 * width, 3 * cf), bf16),
            pltpu.VMEM((5, crows + 2 * narrow, 3 * cc), bf16),
            pltpu.VMEM((5, crows + 2 * narrow, 3 * cc), bf16),
            pltpu.VMEM((rows, cf), f32),
            pltpu.VMEM((crows, cc), f32),
            pltpu.VMEM((levels * width, 128), f32),
            pltpu.VMEM((9, 3 * cf, 2 * cf), bf16),
            pltpu.VMEM((9, 3 * cf, 2 * cf), bf16),
            pltpu.VMEM((9, 3 * cc, 2 * cc), bf16),
            pltpu.VMEM((9, 3 * cc, 2 * cc), bf16),
            pltpu.VMEM((9, 3 * cf, 2 * cc), bf16),
            pltpu.VMEM((rows, 2 * cf), f32),
            pltpu.VMEM((rows // 2, 2 * cf), f32),
            pltpu.VMEM((rows, 2 * cf), f32),
            pltpu.VMEM((rows, 2 * cf), f32),
            pltpu.VMEM((rows // 2, 2 * cf), f32),
            pltpu.VMEM((4, crows, cc), f32),
            pltpu.VMEM((count, levels, cf), f32),
            pltpu.VMEM((count, levels, cf), f32),
            pltpu.VMEM((count, levels, cc), f32),
            pltpu.VMEM((count, levels, cc), f32),
            pltpu.VMEM((rows, 128), f32),
            dma((7,)), dma((7,)),
            dma((count,)), dma((count,)), dma((count,)), dma((count,)),
        ],
        compiler_params=pltpu.CompilerParams(
            collective_id=0, has_side_effects=True, vmem_limit_bytes=40 * 2**20
        ),
        cost_estimate=pl.CostEstimate(flops=10**9, bytes_accessed=6 * 10**6, transcendentals=0),
    )(own, slab, *operands)


def split_weights(w):
    out, inner = w.shape[:2]
    moved = jnp.transpose(w, (2, 3, 4, 1, 0)).reshape(9, 3 * inner, out)
    high = lax.reduce_precision(moved, 8, 7)
    return jnp.concatenate([high, moved - high], axis=2).astype(jnp.bfloat16)


def shifted(value, steps):
    count = lax.axis_size("gx")
    pairs = [(i, i + steps) for i in range(count) if 0 <= i + steps < count]
    return lax.ppermute(value, "gx", pairs)


def per_device(
    fine_in, coarse_in,
    fine_wa, fine_ba, fine_wb, fine_bb,
    coarse_wa, coarse_ba, coarse_wb, coarse_bb,
    down_w, down_b, up_w, up_b,
):
    count = lax.axis_size("gx")
    cf, planes, depth, width = fine_in.shape
    cc, _, levels, narrow = coarse_in.shape
    own = jnp.transpose(fine_in, (1, 2, 3, 0)).reshape(planes, depth * width, cf)
    slab = jnp.transpose(coarse_in, (1, 2, 3, 0)).reshape(1, levels * narrow, cc)
    if depth * width <= ROWS:
        def taps(w, last):
            out, inner = w.shape[:2]
            if last == "in":
                return jnp.transpose(w, (2, 3, 4, 0, 1)).reshape(27, out, inner)
            return jnp.transpose(w, (2, 3, 4, 1, 0)).reshape(27, inner, out)

        fine_sum, coarse_sum = joined_call(
            count, width, narrow, own, slab,
            (
                taps(fine_wa, "in"), fine_ba[None], taps(fine_wb, "in"), fine_bb[None],
                taps(coarse_wa, "in"), coarse_ba[None], taps(coarse_wb, "in"), coarse_bb[None],
                taps(down_w, "out"), down_b[None], up_w, up_b[None],
            ),
        )
        fine_out = jax.nn.gelu(fine_sum.reshape(planes, depth, width, cf), approximate=False)
        coarse_out = jax.nn.gelu(coarse_sum.reshape(levels, narrow, cc), approximate=False)
        return (
            jnp.transpose(fine_out, (3, 0, 1, 2)),
            jnp.transpose(coarse_out, (2, 0, 1))[:, None],
        )
    f7 = jnp.concatenate(
        [shifted(own[1:], 2), shifted(own, 1), own, shifted(own, -1)], axis=0
    )
    c5 = jnp.concatenate(
        [shifted(slab, 2), shifted(slab, 1), slab, shifted(slab, -1), shifted(slab, -2)], axis=0
    )
    up = up_w.T
    up_high = lax.reduce_precision(up, 8, 7)
    wu = jnp.concatenate([up_high, up - up_high], axis=1).astype(jnp.bfloat16)
    frows, crows = depth * width, levels * narrow
    some = max(1, min(levels, ROWS // width))
    vmem = pl.BlockSpec(memory_space=pltpu.VMEM)
    large = frows > 1024
    stage = [pltpu.VMEM((frows, cf), jnp.float32), pltpu.SemaphoreType.DMA] if large else []
    fine, coarse, moved, projected = pl.pallas_call(
        functools.partial(compute, count, width, narrow),
        out_shape=(
            jax.ShapeDtypeStruct((planes, frows, cf), jnp.float32),
            jax.ShapeDtypeStruct((crows, cc), jnp.float32),
            jax.ShapeDtypeStruct((crows, cc), jnp.float32),
            jax.ShapeDtypeStruct((crows, cf), jnp.float32),
        ),
        in_specs=[pl.BlockSpec(memory_space=pl.ANY) if large else vmem] + [vmem] * 13,
        out_specs=(vmem,) * 4,
        scratch_shapes=[
            pltpu.VMEM((7, frows + 2 * width, 3 * cf), jnp.bfloat16),
            pltpu.VMEM((7, frows + 2 * width, 3 * cf), jnp.bfloat16),
            pltpu.VMEM((5, crows + 2 * narrow, 3 * cc), jnp.bfloat16),
            pltpu.VMEM((5, crows + 2 * narrow, 3 * cc), jnp.bfloat16),
            pltpu.VMEM((frows, cf), jnp.float32),
            pltpu.VMEM((crows, cc), jnp.float32),
            pltpu.VMEM((some * width, 128), jnp.float32),
        ] + stage,
        compiler_params=pltpu.CompilerParams(vmem_limit_bytes=(60 if large else 30) * 2**20),
        cost_estimate=pl.CostEstimate(flops=10**9, bytes_accessed=6 * 10**6, transcendentals=0),
    )(
        f7, c5,
        split_weights(fine_wa), fine_ba[None], split_weights(fine_wb), fine_bb[None],
        split_weights(coarse_wa), coarse_ba[None], split_weights(coarse_wb), coarse_bb[None],
        split_weights(down_w), down_b[None], wu, up_b[None],
    )
    both = jnp.concatenate(
        [
            jnp.transpose(moved.reshape(levels, narrow, cc), (1, 0, 2)),
            jnp.transpose(projected.reshape(levels, narrow, cf), (1, 0, 2)),
        ],
        axis=2,
    )
    arrived = lax.all_to_all(both, "gx", split_axis=0, concat_axis=0, tiled=True)
    reduced = jnp.transpose(arrived[:, :, :cc], (1, 0, 2))
    raised = jnp.transpose(arrived[:, :, cc:], (1, 0, 2))
    coarse_out = jax.nn.gelu(coarse.reshape(levels, narrow, cc) + reduced, approximate=False)
    raised = jnp.broadcast_to(
        raised[None, :, None, :, None, :], (planes, levels, depth // levels, narrow, width // narrow, cf)
    ).reshape(planes, depth, width, cf)
    fine_out = jax.nn.gelu(fine.reshape(planes, depth, width, cf) + raised, approximate=False)
    return (
        jnp.transpose(fine_out, (3, 0, 1, 2)),
        jnp.transpose(coarse_out, (2, 0, 1))[:, None],
    )


def solution(mesh):
    split = P(None, ("groups", "gx"), None, None)
    return jax.shard_map(
        per_device,
        mesh=mesh,
        in_specs=(split, split) + (P(),) * 12,
        out_specs=(split, split),
        check_vma=False,
    )
```

```python
import functools

import jax
import jax.numpy as jnp
from jax import lax
from jax.experimental import pallas as pl
from jax.experimental.pallas import tpu as pltpu
from jax.sharding import PartitionSpec as P

ROWS = 512


def halves(value):
    high = value.astype(jnp.bfloat16)
    return high, (value - high.astype(jnp.float32)).astype(jnp.bfloat16)


def put_patches(value, high_ref, low_ref, slot, width, base=None):
    rows, channels = value.shape
    place = lax.rem(lax.broadcasted_iota(jnp.int32, (rows, channels), 0), width)
    before = jnp.where(place == 0, 0.0, pltpu.roll(value, 1, 0))
    after = jnp.where(place == width - 1, 0.0, pltpu.roll(value, rows - 1, 0))
    for k, part in enumerate((before, value, after)):
        high, low = halves(part)
        at = pl.ds(k * channels, channels)
        high_ref[slot, pl.ds(width, rows), at] = high
        low_ref[slot, pl.ds(width, rows), at] = low


def clear_rims(high_ref, low_ref, width):
    slots, rows, lanes = high_ref.shape
    zero = jnp.zeros((slots, width, lanes), jnp.bfloat16)
    for ref in (high_ref, low_ref):
        ref[:, pl.ds(0, width), :] = zero
        ref[:, pl.ds(rows - width, width), :] = zero


def terms(high, low, weights):
    out = weights.shape[1] // 2
    both = jnp.dot(high, weights, preferred_element_type=jnp.float32)
    third = jnp.dot(low, weights[:, :out], preferred_element_type=jnp.float32)
    return both, third


def added(total, pair):
    return pair if total is None else (total[0] + pair[0], total[1] + pair[1])


def folded(pair):
    both, third = pair
    out = third.shape[1]
    return both[:, :out] + both[:, out:] + third


def product(high, low, weights):
    return folded(terms(high, low, weights))


def conv_chunk(high_ref, low_ref, w_ref, slot, start, rows, width):
    total = None
    for p in range(3):
        for q in range(3):
            at = pl.ds(pl.multiple_of(start + q * width, 16), rows)
            total = added(
                total,
                terms(high_ref[slot + p, at, :], low_ref[slot + p, at, :], w_ref[3 * p + q]),
            )
    return folded(total)


def conv_plane(high_ref, low_ref, w_ref, temp_ref, slot, width, finish):
    rows = temp_ref.shape[0]
    step = min(ROWS, rows)

    def body(i, _):
        start = i * step
        at = pl.ds(pl.multiple_of(start, 16), step)
        temp_ref[at, :] = finish(
            conv_chunk(high_ref, low_ref, w_ref, slot, start, step, width), at
        )
        return 0

    if rows == step:
        temp_ref[...] = finish(
            conv_chunk(high_ref, low_ref, w_ref, slot, 0, step, width), pl.ds(0, step)
        )
    else:
        lax.fori_loop(0, rows // step, body, 0)


def compute(
    count, width, narrow,
    f7, c5, wfa, bfa, wfb, bfb, wca, bca, wcb, bcb, wd, bd, wu, bu,
    fine_ref, coarse_ref, moved_ref, projected_ref,
    fhi, flo, chi, clo, ftemp, ctemp, mtemp, *staged,
):
    me = lax.axis_index("gx")

    def plane_of(j):
        if not staged:
            return f7.at[j]
        copy = pltpu.make_async_copy(f7.at[j], staged[0], staged[1])
        copy.start()
        copy.wait()
        return staged[0]

    clear_rims(chi, clo, narrow)

    def coarse_load(j, _):
        put_patches(c5[j], chi, clo, j, narrow)
        return 0

    lax.fori_loop(0, 5, coarse_load, 0)

    def coarse_mid(j, _):
        y = me - 1 + j
        inside = jnp.where((y >= 0) & (y < count), 1.0, 0.0)
        conv_plane(
            chi, clo, wca, ctemp, j, narrow,
            lambda total, at: jnp.maximum(total + bca[...], 0.0) * inside,
        )
        put_patches(ctemp[...], chi, clo, j, narrow)
        return 0

    lax.fori_loop(0, 3, coarse_mid, 0)
    conv_plane(
        chi, clo, wcb, ctemp, 0, narrow,
        lambda total, at: jnp.maximum(c5[2, at, :] + total + bcb[...], 0.0),
    )
    coarse = ctemp[...]
    coarse_ref[...] = coarse
    projected_ref[...] = product(*halves(coarse), wu[...]) + bu[...]

    clear_rims(fhi, flo, width)

    def fine_load(j, _):
        put_patches(plane_of(j)[...], fhi, flo, j, width)
        return 0

    lax.fori_loop(0, 7, fine_load, 0)

    def fine_mid(j, _):
        x = 2 * me - 2 + j
        inside = jnp.where((x >= 0) & (x < 2 * count), 1.0, 0.0)
        conv_plane(
            fhi, flo, wfa, ftemp, j, width,
            lambda total, at: jnp.maximum(total + bfa[...], 0.0) * inside,
        )
        put_patches(ftemp[...], fhi, flo, j, width)
        return 0

    lax.fori_loop(0, 5, fine_mid, 0)

    def fine_last(j, _):
        x = 2 * me - 1 + j
        inside = jnp.where(x >= 0, 1.0, 0.0)
        own = plane_of(j + 2)
        conv_plane(
            fhi, flo, wfb, ftemp, j, width,
            lambda total, at: jnp.maximum(own[at, :] + total + bfb[...], 0.0) * inside,
        )
        fine = ftemp[...]
        put_patches(fine, fhi, flo, j, width)
        fine_ref[jnp.maximum(j - 1, 0)] = fine
        return 0

    lax.fori_loop(0, 3, fine_last, 0)

    levels = moved_ref.shape[0] // narrow
    some = max(1, min(levels, ROWS // width))
    for first in range(0, levels, some):
        total = None
        for p in range(3):
            for q in range(3):
                def rows_of(ref):
                    return jnp.concatenate(
                        [ref[p, pl.ds((2 * b + q) * width, width), :] for b in range(first, first + some)],
                        axis=0,
                    )
                total = added(total, terms(rows_of(fhi), rows_of(flo), wd[3 * p + q]))
        total = folded(total)
        channels = total.shape[1]
        mtemp[:, pl.ds(0, channels)] = total + bd[...]
        moved_ref[pl.ds(first * narrow, some * narrow), :] = mtemp[
            pl.ds(0, some * narrow, stride=2), :
        ][:, :channels]


def prepare(raw_ref, out_ref, transposed):
    def body(t, _):
        for r in range(3):
            w = raw_ref[3 * t + r]
            if transposed:
                w = w.T
            high, low = halves(w)
            inner, out = w.shape
            out_ref[t, pl.ds(r * inner, inner), pl.ds(0, out)] = high
            out_ref[t, pl.ds(r * inner, inner), pl.ds(out, out)] = low
        return 0

    lax.fori_loop(0, 9, body, 0)


def joined(
    count, width, narrow,
    *refs,
):
    sources, (fine_ref, coarse_ref) = refs[:14], refs[14:16]
    local, fetched = refs[16:30], refs[30]
    joined_body(count, width, narrow, sources, local, fetched, fine_ref, coarse_ref, *refs[31:])


def joined_body(
    count, width, narrow, sources, local, fetched, fine_ref, coarse_ref,
    fhi, flo, chi, clo, ftemp, ctemp, mtemp,
    wfa, wfb, wca, wcb, wd,
    pair_send, half_send, pair_low, pair_high, half_low, crecv,
    psend, precv, msend, mrecv, spread,
    hs, hr, ps, pr, ms, mr,
):
    own, slab, rfa, bfa, rfb, bfb, rca, bca, rcb, bcb, rd, bd, up, bu = local

    def fetch(k):
        return pltpu.make_async_copy(sources[k], local[k], fetched.at[k])

    me = lax.axis_index("gx")
    mesh_id = pl.DeviceIdType.MESH
    rows, cf = ftemp.shape
    cc = ctemp.shape[1]
    levels = ctemp.shape[0] // narrow
    half = rows // 2
    barrier = pltpu.get_barrier_semaphore()

    def greet(k, _):
        pl.semaphore_signal(
            barrier, inc=1, device_id={"gx": lax.rem(me + k, count)}, device_id_type=mesh_id
        )
        return 0

    lax.fori_loop(1, count, greet, 0)
    for k in (1, 0, 6, 7, 8, 9, 2, 3, 12, 13, 4, 5, 10, 11):
        fetch(k).start()
    fetch(1).wait()
    fetch(0).wait()

    pair_send[:, pl.ds(0, cf)] = own[0]
    pair_send[:, pl.ds(cf, cf)] = own[1]
    half_send[:, pl.ds(0, cf)] = own[1, pl.ds(0, half), :]
    half_send[:, pl.ds(cf, cf)] = own[1, pl.ds(half, half), :]
    pl.semaphore_wait(barrier, count - 1)

    halos = (
        (slab.at[0], crecv.at[1], 1),
        (slab.at[0], crecv.at[2], -1),
        (slab.at[0], crecv.at[0], 2),
        (slab.at[0], crecv.at[3], -2),
        (pair_send, pair_low, 1),
        (pair_send, pair_high, -1),
        (half_send, half_low, 2),
    )

    def copy_of(k):
        source, target, step = halos[k]
        return pltpu.make_async_remote_copy(
            src_ref=source, dst_ref=target, send_sem=hs.at[k], recv_sem=hr.at[k],
            device_id={"gx": lax.rem(me + step + count, count)}, device_id_type=mesh_id,
        )

    def sends(k):
        step = halos[k][2]
        return (me + step >= 0) & (me + step < count)

    def receives(k):
        step = halos[k][2]
        return (me - step >= 0) & (me - step < count)

    for k in range(7):
        @pl.when(sends(k))
        def _():
            copy_of(k).start()

        @pl.when(jnp.logical_not(receives(k)))
        def _():
            target = halos[k][1]
            target[...] = jnp.zeros(target.shape, jnp.float32)

    clear_rims(chi, clo, narrow)
    clear_rims(fhi, flo, width)
    for k in range(2, 14):
        fetch(k).wait()
    prepare(rca, wca, True)
    prepare(rcb, wcb, True)
    put_patches(slab[0], chi, clo, 2, narrow)

    def landed(k):
        @pl.when(receives(k))
        def _():
            copy_of(k).wait_recv()

    for k in range(4):
        landed(k)
    for k, slot in enumerate((0, 1, 3, 4)):
        put_patches(crecv[k], chi, clo, slot, narrow)

    def coarse_mid(j, _):
        y = me - 1 + j
        inside = jnp.where((y >= 0) & (y < count), 1.0, 0.0)
        conv_plane(
            chi, clo, wca, ctemp, j, narrow,
            lambda total, at: jnp.maximum(total + bca[...], 0.0) * inside,
        )
        put_patches(ctemp[...], chi, clo, j, narrow)
        return 0

    lax.fori_loop(0, 3, coarse_mid, 0)
    conv_plane(
        chi, clo, wcb, ctemp, 0, narrow,
        lambda total, at: jnp.maximum(slab[0, at, :] + total + bcb[...], 0.0),
    )
    uh, ul = halves(up[...].T)
    projected = product(*halves(ctemp[...]), jnp.concatenate([uh, ul], axis=1)) + bu[...]
    for d in range(levels):
        psend[:, d, :] = projected[d * narrow : (d + 1) * narrow]

    def exchange(send, recv, send_sem, recv_sem, k):
        target = lax.rem(me + k, count)
        return pltpu.make_async_remote_copy(
            src_ref=send.at[target], dst_ref=recv.at[me],
            send_sem=send_sem.at[k], recv_sem=recv_sem.at[k],
            device_id={"gx": target}, device_id_type=mesh_id,
        )

    def start_all(send, recv, send_sem, recv_sem):
        def body(k, _):
            exchange(send, recv, send_sem, recv_sem, k).start()
            return 0

        lax.fori_loop(1, count, body, 0)
        recv[me] = send[me]

    def wait_all(send, recv, send_sem, recv_sem):
        def body(k, _):
            source = lax.rem(me - k + count, count)
            pltpu.make_async_remote_copy(
                src_ref=send.at[source], dst_ref=recv.at[source],
                send_sem=send_sem.at[k], recv_sem=recv_sem.at[k],
                device_id={"gx": source}, device_id_type=mesh_id,
            ).wait_recv()
            exchange(send, recv, send_sem, recv_sem, k).wait_send()
            return 0

        lax.fori_loop(1, count, body, 0)

    start_all(psend, precv, ps, pr)

    prepare(rfa, wfa, True)
    put_patches(own[0], fhi, flo, 3, width)
    put_patches(own[1], fhi, flo, 4, width)
    for k in range(4, 7):
        landed(k)
    put_patches(
        jnp.concatenate([half_low[:, pl.ds(0, cf)], half_low[:, pl.ds(cf, cf)]], axis=0),
        fhi, flo, 0, width,
    )
    put_patches(pair_low[:, pl.ds(0, cf)], fhi, flo, 1, width)
    put_patches(pair_low[:, pl.ds(cf, cf)], fhi, flo, 2, width)
    put_patches(pair_high[:, pl.ds(0, cf)], fhi, flo, 5, width)
    put_patches(pair_high[:, pl.ds(cf, cf)], fhi, flo, 6, width)

    def fine_mid(j, _):
        x = 2 * me - 2 + j
        inside = jnp.where((x >= 0) & (x < 2 * count), 1.0, 0.0)
        conv_plane(
            fhi, flo, wfa, ftemp, j, width,
            lambda total, at: jnp.maximum(total + bfa[...], 0.0) * inside,
        )
        put_patches(ftemp[...], fhi, flo, j, width)
        return 0

    lax.fori_loop(0, 5, fine_mid, 0)
    prepare(rfb, wfb, True)
    prepare(rd, wd, False)
    before = jnp.where(me > 0, 1.0, 0.0)
    conv_plane(
        fhi, flo, wfb, ftemp, 0, width,
        lambda total, at: jnp.maximum(pair_low[at, pl.ds(cf, cf)] + total + bfb[...], 0.0) * before,
    )
    put_patches(ftemp[...], fhi, flo, 0, width)

    def fine_last(j, _):
        conv_plane(
            fhi, flo, wfb, ftemp, j, width,
            lambda total, at: jnp.maximum(own[j - 1, at, :] + total + bfb[...], 0.0),
        )
        put_patches(ftemp[...], fhi, flo, j, width)
        fine_ref[j - 1] = ftemp[...]
        return 0

    lax.fori_loop(1, 3, fine_last, 0)

    total = None
    for p in range(3):
        for q in range(3):
            def rows_of(ref):
                return jnp.concatenate(
                    [ref[p, pl.ds((2 * b + q) * width, width), :] for b in range(levels)], axis=0
                )
            total = added(total, terms(rows_of(fhi), rows_of(flo), wd[3 * p + q]))
    total = folded(total)
    mtemp[:, pl.ds(0, cc)] = total + bd[...]
    for b in range(levels):
        msend[:, b, :] = mtemp[pl.ds(b * width, narrow, stride=2), :][:, :cc]
    start_all(msend, mrecv, ms, mr)

    wait_all(psend, precv, ps, pr)
    for d in range(rows // width):
        block = precv[:, d // 2, :]
        for s in range(2):
            spread[pl.ds(d * width + s, narrow, stride=2), pl.ds(0, cf)] = block
    for x in range(2):
        fine_ref[x] = fine_ref[x] + spread[:, pl.ds(0, cf)]
    for k in range(7):
        @pl.when(sends(k))
        def _():
            copy_of(k).wait_send()

    wait_all(msend, mrecv, ms, mr)
    for d in range(levels):
        at = pl.ds(d * narrow, narrow)
        coarse_ref[at, :] = ctemp[at, :] + mrecv[:, d, :]


def joined_call(count, width, narrow, own, slab, operands):
    planes, rows, cf = own.shape
    _, crows, cc = slab.shape
    levels = crows // narrow
    f32, bf16 = jnp.float32, jnp.bfloat16
    vmem = pl.BlockSpec(memory_space=pltpu.VMEM)
    dma = pltpu.SemaphoreType.DMA
    return pl.pallas_call(
        functools.partial(joined, count, width, narrow),
        out_shape=(
            jax.ShapeDtypeStruct((planes, rows, cf), f32),
            jax.ShapeDtypeStruct((crows, cc), f32),
        ),
        in_specs=[pl.BlockSpec(memory_space=pl.ANY)] * 14,
        out_specs=(vmem,) * 2,
        scratch_shapes=[pltpu.VMEM(v.shape, f32) for v in (own, slab) + operands]
        + [
            dma((14,)),
            pltpu.VMEM((7, rows + 2 * width, 3 * cf), bf16),
            pltpu.VMEM((7, rows + 2 * width, 3 * cf), bf16),
            pltpu.VMEM((5, crows + 2 * narrow, 3 * cc), bf16),
            pltpu.VMEM((5, crows + 2 * narrow, 3 * cc), bf16),
            pltpu.VMEM((rows, cf), f32),
            pltpu.VMEM((crows, cc), f32),
            pltpu.VMEM((levels * width, 128), f32),
            pltpu.VMEM((9, 3 * cf, 2 * cf), bf16),
            pltpu.VMEM((9, 3 * cf, 2 * cf), bf16),
            pltpu.VMEM((9, 3 * cc, 2 * cc), bf16),
            pltpu.VMEM((9, 3 * cc, 2 * cc), bf16),
            pltpu.VMEM((9, 3 * cf, 2 * cc), bf16),
            pltpu.VMEM((rows, 2 * cf), f32),
            pltpu.VMEM((rows // 2, 2 * cf), f32),
            pltpu.VMEM((rows, 2 * cf), f32),
            pltpu.VMEM((rows, 2 * cf), f32),
            pltpu.VMEM((rows // 2, 2 * cf), f32),
            pltpu.VMEM((4, crows, cc), f32),
            pltpu.VMEM((count, levels, cf), f32),
            pltpu.VMEM((count, levels, cf), f32),
            pltpu.VMEM((count, levels, cc), f32),
            pltpu.VMEM((count, levels, cc), f32),
            pltpu.VMEM((rows, 128), f32),
            dma((7,)), dma((7,)),
            dma((count,)), dma((count,)), dma((count,)), dma((count,)),
        ],
        compiler_params=pltpu.CompilerParams(
            collective_id=0, has_side_effects=True, vmem_limit_bytes=60 * 2**20
        ),
        cost_estimate=pl.CostEstimate(flops=10**9, bytes_accessed=6 * 10**6, transcendentals=0),
    )(own, slab, *operands)


def split_weights(w):
    out, inner = w.shape[:2]
    moved = jnp.transpose(w, (2, 3, 4, 1, 0)).reshape(9, 3 * inner, out)
    high = lax.reduce_precision(moved, 8, 7)
    return jnp.concatenate([high, moved - high], axis=2).astype(jnp.bfloat16)


def shifted(value, steps):
    count = lax.axis_size("gx")
    pairs = [(i, i + steps) for i in range(count) if 0 <= i + steps < count]
    return lax.ppermute(value, "gx", pairs)


def per_device(
    fine_in, coarse_in,
    fine_wa, fine_ba, fine_wb, fine_bb,
    coarse_wa, coarse_ba, coarse_wb, coarse_bb,
    down_w, down_b, up_w, up_b,
):
    count = lax.axis_size("gx")
    cf, planes, depth, width = fine_in.shape
    cc, _, levels, narrow = coarse_in.shape
    own = jnp.transpose(fine_in, (1, 2, 3, 0)).reshape(planes, depth * width, cf)
    slab = jnp.transpose(coarse_in, (1, 2, 3, 0)).reshape(1, levels * narrow, cc)
    if depth * width <= ROWS:
        def taps(w, last):
            out, inner = w.shape[:2]
            if last == "in":
                return jnp.transpose(w, (2, 3, 4, 0, 1)).reshape(27, out, inner)
            return jnp.transpose(w, (2, 3, 4, 1, 0)).reshape(27, inner, out)

        fine_sum, coarse_sum = joined_call(
            count, width, narrow, own, slab,
            (
                taps(fine_wa, "in"), fine_ba[None], taps(fine_wb, "in"), fine_bb[None],
                taps(coarse_wa, "in"), coarse_ba[None], taps(coarse_wb, "in"), coarse_bb[None],
                taps(down_w, "out"), down_b[None], up_w, up_b[None],
            ),
        )
        fine_out = jax.nn.gelu(fine_sum.reshape(planes, depth, width, cf), approximate=False)
        coarse_out = jax.nn.gelu(coarse_sum.reshape(levels, narrow, cc), approximate=False)
        return (
            jnp.transpose(fine_out, (3, 0, 1, 2)),
            jnp.transpose(coarse_out, (2, 0, 1))[:, None],
        )
    f7 = jnp.concatenate(
        [shifted(own[1:], 2), shifted(own, 1), own, shifted(own, -1)], axis=0
    )
    c5 = jnp.concatenate(
        [shifted(slab, 2), shifted(slab, 1), slab, shifted(slab, -1), shifted(slab, -2)], axis=0
    )
    up = up_w.T
    up_high = lax.reduce_precision(up, 8, 7)
    wu = jnp.concatenate([up_high, up - up_high], axis=1).astype(jnp.bfloat16)
    frows, crows = depth * width, levels * narrow
    some = max(1, min(levels, ROWS // width))
    vmem = pl.BlockSpec(memory_space=pltpu.VMEM)
    large = frows > 1024
    stage = [pltpu.VMEM((frows, cf), jnp.float32), pltpu.SemaphoreType.DMA] if large else []
    fine, coarse, moved, projected = pl.pallas_call(
        functools.partial(compute, count, width, narrow),
        out_shape=(
            jax.ShapeDtypeStruct((planes, frows, cf), jnp.float32),
            jax.ShapeDtypeStruct((crows, cc), jnp.float32),
            jax.ShapeDtypeStruct((crows, cc), jnp.float32),
            jax.ShapeDtypeStruct((crows, cf), jnp.float32),
        ),
        in_specs=[pl.BlockSpec(memory_space=pl.ANY) if large else vmem] + [vmem] * 13,
        out_specs=(vmem,) * 4,
        scratch_shapes=[
            pltpu.VMEM((7, frows + 2 * width, 3 * cf), jnp.bfloat16),
            pltpu.VMEM((7, frows + 2 * width, 3 * cf), jnp.bfloat16),
            pltpu.VMEM((5, crows + 2 * narrow, 3 * cc), jnp.bfloat16),
            pltpu.VMEM((5, crows + 2 * narrow, 3 * cc), jnp.bfloat16),
            pltpu.VMEM((frows, cf), jnp.float32),
            pltpu.VMEM((crows, cc), jnp.float32),
            pltpu.VMEM((some * width, 128), jnp.float32),
        ] + stage,
        compiler_params=pltpu.CompilerParams(vmem_limit_bytes=(60 if large else 30) * 2**20),
        cost_estimate=pl.CostEstimate(flops=10**9, bytes_accessed=6 * 10**6, transcendentals=0),
    )(
        f7, c5,
        split_weights(fine_wa), fine_ba[None], split_weights(fine_wb), fine_bb[None],
        split_weights(coarse_wa), coarse_ba[None], split_weights(coarse_wb), coarse_bb[None],
        split_weights(down_w), down_b[None], wu, up_b[None],
    )
    both = jnp.concatenate(
        [
            jnp.transpose(moved.reshape(levels, narrow, cc), (1, 0, 2)),
            jnp.transpose(projected.reshape(levels, narrow, cf), (1, 0, 2)),
        ],
        axis=2,
    )
    arrived = lax.all_to_all(both, "gx", split_axis=0, concat_axis=0, tiled=True)
    reduced = jnp.transpose(arrived[:, :, :cc], (1, 0, 2))
    raised = jnp.transpose(arrived[:, :, cc:], (1, 0, 2))
    coarse_out = jax.nn.gelu(coarse.reshape(levels, narrow, cc) + reduced, approximate=False)
    raised = jnp.broadcast_to(
        raised[None, :, None, :, None, :], (planes, levels, depth // levels, narrow, width // narrow, cf)
    ).reshape(planes, depth, width, cf)
    fine_out = jax.nn.gelu(fine.reshape(planes, depth, width, cf) + raised, approximate=False)
    return (
        jnp.transpose(fine_out, (3, 0, 1, 2)),
        jnp.transpose(coarse_out, (2, 0, 1))[:, None],
    )


def solution(mesh):
    split = P(None, ("groups", "gx"), None, None)
    return jax.shard_map(
        per_device,
        mesh=mesh,
        in_specs=(split, split) + (P(),) * 12,
        out_specs=(split, split),
        check_vma=False,
    )
```

```python
import functools

import jax
import jax.numpy as jnp
from jax import lax
from jax.experimental import pallas as pl
from jax.experimental.pallas import tpu as pltpu
from jax.sharding import PartitionSpec as P

ROWS = 512


def halves(value):
    high = value.astype(jnp.bfloat16)
    return high, (value - high.astype(jnp.float32)).astype(jnp.bfloat16)


def put_patches(value, high_ref, low_ref, slot, width, base=None):
    rows, channels = value.shape
    place = lax.rem(lax.broadcasted_iota(jnp.int32, (rows, channels), 0), width)
    before = jnp.where(place == 0, 0.0, pltpu.roll(value, 1, 0))
    after = jnp.where(place == width - 1, 0.0, pltpu.roll(value, rows - 1, 0))
    for k, part in enumerate((before, value, after)):
        high, low = halves(part)
        at = pl.ds(k * channels, channels)
        high_ref[slot, pl.ds(width, rows), at] = high
        low_ref[slot, pl.ds(width, rows), at] = low


def clear_rims(high_ref, low_ref, width):
    slots, rows, lanes = high_ref.shape
    zero = jnp.zeros((slots, width, lanes), jnp.bfloat16)
    for ref in (high_ref, low_ref):
        ref[:, pl.ds(0, width), :] = zero
        ref[:, pl.ds(rows - width, width), :] = zero


def terms(high, low, weights):
    out = weights.shape[1] // 2
    both = jnp.dot(high, weights, preferred_element_type=jnp.float32)
    third = jnp.dot(low, weights[:, :out], preferred_element_type=jnp.float32)
    return both, third


def added(total, pair):
    return pair if total is None else (total[0] + pair[0], total[1] + pair[1])


def folded(pair):
    both, third = pair
    out = third.shape[1]
    return both[:, :out] + both[:, out:] + third


def product(high, low, weights):
    return folded(terms(high, low, weights))


def conv_chunk(high_ref, low_ref, w_ref, slot, start, rows, width):
    total = None
    for p in range(3):
        for q in range(3):
            at = pl.ds(pl.multiple_of(start + q * width, 16), rows)
            total = added(
                total,
                terms(high_ref[slot + p, at, :], low_ref[slot + p, at, :], w_ref[3 * p + q]),
            )
    return folded(total)


def conv_plane(high_ref, low_ref, w_ref, temp_ref, slot, width, finish):
    rows = temp_ref.shape[0]
    step = min(ROWS, rows)

    def body(i, _):
        start = i * step
        at = pl.ds(pl.multiple_of(start, 16), step)
        temp_ref[at, :] = finish(
            conv_chunk(high_ref, low_ref, w_ref, slot, start, step, width), at
        )
        return 0

    if rows == step:
        temp_ref[...] = finish(
            conv_chunk(high_ref, low_ref, w_ref, slot, 0, step, width), pl.ds(0, step)
        )
    else:
        lax.fori_loop(0, rows // step, body, 0)


def compute(
    count, width, narrow,
    f7, c5, wfa, bfa, wfb, bfb, wca, bca, wcb, bcb, wd, bd, wu, bu,
    fine_ref, coarse_ref, moved_ref, projected_ref,
    fhi, flo, chi, clo, ftemp, ctemp, mtemp, *staged,
):
    me = lax.axis_index("gx")

    def plane_of(j):
        if not staged:
            return f7.at[j]
        copy = pltpu.make_async_copy(f7.at[j], staged[0], staged[1])
        copy.start()
        copy.wait()
        return staged[0]

    clear_rims(chi, clo, narrow)

    def coarse_load(j, _):
        put_patches(c5[j], chi, clo, j, narrow)
        return 0

    lax.fori_loop(0, 5, coarse_load, 0)

    def coarse_mid(j, _):
        y = me - 1 + j
        inside = jnp.where((y >= 0) & (y < count), 1.0, 0.0)
        conv_plane(
            chi, clo, wca, ctemp, j, narrow,
            lambda total, at: jnp.maximum(total + bca[...], 0.0) * inside,
        )
        put_patches(ctemp[...], chi, clo, j, narrow)
        return 0

    lax.fori_loop(0, 3, coarse_mid, 0)
    conv_plane(
        chi, clo, wcb, ctemp, 0, narrow,
        lambda total, at: jnp.maximum(c5[2, at, :] + total + bcb[...], 0.0),
    )
    coarse = ctemp[...]
    coarse_ref[...] = coarse
    projected_ref[...] = product(*halves(coarse), wu[...]) + bu[...]

    clear_rims(fhi, flo, width)

    def fine_load(j, _):
        put_patches(plane_of(j)[...], fhi, flo, j, width)
        return 0

    lax.fori_loop(0, 7, fine_load, 0)

    def fine_mid(j, _):
        x = 2 * me - 2 + j
        inside = jnp.where((x >= 0) & (x < 2 * count), 1.0, 0.0)
        conv_plane(
            fhi, flo, wfa, ftemp, j, width,
            lambda total, at: jnp.maximum(total + bfa[...], 0.0) * inside,
        )
        put_patches(ftemp[...], fhi, flo, j, width)
        return 0

    lax.fori_loop(0, 5, fine_mid, 0)

    def fine_last(j, _):
        x = 2 * me - 1 + j
        inside = jnp.where(x >= 0, 1.0, 0.0)
        own = plane_of(j + 2)
        conv_plane(
            fhi, flo, wfb, ftemp, j, width,
            lambda total, at: jnp.maximum(own[at, :] + total + bfb[...], 0.0) * inside,
        )
        fine = ftemp[...]
        put_patches(fine, fhi, flo, j, width)
        fine_ref[jnp.maximum(j - 1, 0)] = fine
        return 0

    lax.fori_loop(0, 3, fine_last, 0)

    levels = moved_ref.shape[0] // narrow
    some = max(1, min(levels, ROWS // width))
    for first in range(0, levels, some):
        total = None
        for p in range(3):
            for q in range(3):
                def rows_of(ref):
                    return jnp.concatenate(
                        [ref[p, pl.ds((2 * b + q) * width, width), :] for b in range(first, first + some)],
                        axis=0,
                    )
                total = added(total, terms(rows_of(fhi), rows_of(flo), wd[3 * p + q]))
        total = folded(total)
        channels = total.shape[1]
        mtemp[:, pl.ds(0, channels)] = total + bd[...]
        moved_ref[pl.ds(first * narrow, some * narrow), :] = mtemp[
            pl.ds(0, some * narrow, stride=2), :
        ][:, :channels]


def prepare(raw_ref, out_ref, transposed):
    def body(t, _):
        for r in range(3):
            w = raw_ref[3 * t + r]
            if transposed:
                w = w.T
            high, low = halves(w)
            inner, out = w.shape
            out_ref[t, pl.ds(r * inner, inner), pl.ds(0, out)] = high
            out_ref[t, pl.ds(r * inner, inner), pl.ds(out, out)] = low
        return 0

    lax.fori_loop(0, 9, body, 0)


def joined(
    count, width, narrow,
    *refs,
):
    sources, (fine_ref, coarse_ref) = refs[:14], refs[14:16]
    local, fetched = refs[16:30], refs[30]
    joined_body(count, width, narrow, sources, local, fetched, fine_ref, coarse_ref, *refs[31:])


def joined_body(
    count, width, narrow, sources, local, fetched, fine_ref, coarse_ref,
    fhi, flo, chi, clo, ftemp, ctemp, mtemp,
    wfa, wfb, wca, wcb, wd,
    pair_send, half_send, pair_low, pair_high, half_low, crecv,
    psend, precv, msend, mrecv, spread,
    hs, hr, ps, pr, ms, mr,
):
    own, slab, rfa, bfa, rfb, bfb, rca, bca, rcb, bcb, rd, bd, up, bu = local

    def fetch(k):
        return pltpu.make_async_copy(sources[k], local[k], fetched.at[k])

    me = lax.axis_index("gx")
    mesh_id = pl.DeviceIdType.MESH
    rows, cf = ftemp.shape
    cc = ctemp.shape[1]
    levels = ctemp.shape[0] // narrow
    half = rows // 2
    barrier = pltpu.get_barrier_semaphore()

    def greet(k, _):
        pl.semaphore_signal(
            barrier, inc=1, device_id={"gx": lax.rem(me + k, count)}, device_id_type=mesh_id
        )
        return 0

    lax.fori_loop(1, count, greet, 0)
    for k in (1, 0, 6, 7, 8, 9, 2, 3, 12, 13, 4, 5, 10, 11):
        fetch(k).start()
    fetch(1).wait()
    fetch(0).wait()

    pair_send[:, pl.ds(0, cf)] = own[0]
    pair_send[:, pl.ds(cf, cf)] = own[1]
    half_send[:, pl.ds(0, cf)] = own[1, pl.ds(0, half), :]
    half_send[:, pl.ds(cf, cf)] = own[1, pl.ds(half, half), :]
    pl.semaphore_wait(barrier, count - 1)

    halos = (
        (slab.at[0], crecv.at[1], 1),
        (slab.at[0], crecv.at[2], -1),
        (slab.at[0], crecv.at[0], 2),
        (slab.at[0], crecv.at[3], -2),
        (pair_send, pair_low, 1),
        (pair_send, pair_high, -1),
        (half_send, half_low, 2),
    )

    def copy_of(k):
        source, target, step = halos[k]
        return pltpu.make_async_remote_copy(
            src_ref=source, dst_ref=target, send_sem=hs.at[k], recv_sem=hr.at[k],
            device_id={"gx": lax.rem(me + step + count, count)}, device_id_type=mesh_id,
        )

    def sends(k):
        step = halos[k][2]
        return (me + step >= 0) & (me + step < count)

    def receives(k):
        step = halos[k][2]
        return (me - step >= 0) & (me - step < count)

    for k in range(7):
        @pl.when(sends(k))
        def _():
            copy_of(k).start()

        @pl.when(jnp.logical_not(receives(k)))
        def _():
            target = halos[k][1]
            target[...] = jnp.zeros(target.shape, jnp.float32)

    clear_rims(chi, clo, narrow)
    clear_rims(fhi, flo, width)
    for k in range(2, 14):
        fetch(k).wait()
    prepare(rca, wca, True)
    prepare(rcb, wcb, True)
    put_patches(slab[0], chi, clo, 2, narrow)

    prepare(rfa, wfa, True)
    prepare(rfb, wfb, True)
    prepare(rd, wd, False)
    put_patches(own[0], fhi, flo, 3, width)
    put_patches(own[1], fhi, flo, 4, width)

    def landed(k):
        @pl.when(receives(k))
        def _():
            copy_of(k).wait_recv()

    for k in range(4):
        landed(k)
    for k, slot in enumerate((0, 1, 3, 4)):
        put_patches(crecv[k], chi, clo, slot, narrow)

    def coarse_mid(j, _):
        y = me - 1 + j
        inside = jnp.where((y >= 0) & (y < count), 1.0, 0.0)
        conv_plane(
            chi, clo, wca, ctemp, j, narrow,
            lambda total, at: jnp.maximum(total + bca[...], 0.0) * inside,
        )
        put_patches(ctemp[...], chi, clo, j, narrow)
        return 0

    lax.fori_loop(0, 3, coarse_mid, 0)
    conv_plane(
        chi, clo, wcb, ctemp, 0, narrow,
        lambda total, at: jnp.maximum(slab[0, at, :] + total + bcb[...], 0.0),
    )
    uh, ul = halves(up[...].T)
    projected = product(*halves(ctemp[...]), jnp.concatenate([uh, ul], axis=1)) + bu[...]
    for d in range(levels):
        psend[:, d, :] = projected[d * narrow : (d + 1) * narrow]

    def exchange(send, recv, send_sem, recv_sem, k):
        target = lax.rem(me + k, count)
        return pltpu.make_async_remote_copy(
            src_ref=send.at[target], dst_ref=recv.at[me],
            send_sem=send_sem.at[k], recv_sem=recv_sem.at[k],
            device_id={"gx": target}, device_id_type=mesh_id,
        )

    def start_all(send, recv, send_sem, recv_sem):
        def body(k, _):
            exchange(send, recv, send_sem, recv_sem, k).start()
            return 0

        lax.fori_loop(1, count, body, 0)
        recv[me] = send[me]

    def wait_all(send, recv, send_sem, recv_sem):
        def body(k, _):
            source = lax.rem(me - k + count, count)
            pltpu.make_async_remote_copy(
                src_ref=send.at[source], dst_ref=recv.at[source],
                send_sem=send_sem.at[k], recv_sem=recv_sem.at[k],
                device_id={"gx": source}, device_id_type=mesh_id,
            ).wait_recv()
            exchange(send, recv, send_sem, recv_sem, k).wait_send()
            return 0

        lax.fori_loop(1, count, body, 0)

    start_all(psend, precv, ps, pr)

    for k in range(4, 7):
        landed(k)
    put_patches(
        jnp.concatenate([half_low[:, pl.ds(0, cf)], half_low[:, pl.ds(cf, cf)]], axis=0),
        fhi, flo, 0, width,
    )
    put_patches(pair_low[:, pl.ds(0, cf)], fhi, flo, 1, width)
    put_patches(pair_low[:, pl.ds(cf, cf)], fhi, flo, 2, width)
    put_patches(pair_high[:, pl.ds(0, cf)], fhi, flo, 5, width)
    put_patches(pair_high[:, pl.ds(cf, cf)], fhi, flo, 6, width)

    def fine_mid(j, _):
        x = 2 * me - 2 + j
        inside = jnp.where((x >= 0) & (x < 2 * count), 1.0, 0.0)
        conv_plane(
            fhi, flo, wfa, ftemp, j, width,
            lambda total, at: jnp.maximum(total + bfa[...], 0.0) * inside,
        )
        put_patches(ftemp[...], fhi, flo, j, width)
        return 0

    lax.fori_loop(0, 5, fine_mid, 0)
    before = jnp.where(me > 0, 1.0, 0.0)
    conv_plane(
        fhi, flo, wfb, ftemp, 0, width,
        lambda total, at: jnp.maximum(pair_low[at, pl.ds(cf, cf)] + total + bfb[...], 0.0) * before,
    )
    put_patches(ftemp[...], fhi, flo, 0, width)

    def fine_last(j, _):
        conv_plane(
            fhi, flo, wfb, ftemp, j, width,
            lambda total, at: jnp.maximum(own[j - 1, at, :] + total + bfb[...], 0.0),
        )
        put_patches(ftemp[...], fhi, flo, j, width)
        fine_ref[j - 1] = ftemp[...]
        return 0

    lax.fori_loop(1, 3, fine_last, 0)

    total = None
    for p in range(3):
        for q in range(3):
            def rows_of(ref):
                return jnp.concatenate(
                    [ref[p, pl.ds((2 * b + q) * width, width), :] for b in range(levels)], axis=0
                )
            total = added(total, terms(rows_of(fhi), rows_of(flo), wd[3 * p + q]))
    total = folded(total)
    mtemp[:, pl.ds(0, cc)] = total + bd[...]
    for b in range(levels):
        msend[:, b, :] = mtemp[pl.ds(b * width, narrow, stride=2), :][:, :cc]
    start_all(msend, mrecv, ms, mr)

    wait_all(psend, precv, ps, pr)
    for d in range(rows // width):
        block = precv[:, d // 2, :]
        for s in range(2):
            spread[pl.ds(d * width + s, narrow, stride=2), pl.ds(0, cf)] = block
    for x in range(2):
        fine_ref[x] = fine_ref[x] + spread[:, pl.ds(0, cf)]
    for k in range(7):
        @pl.when(sends(k))
        def _():
            copy_of(k).wait_send()

    wait_all(msend, mrecv, ms, mr)
    for d in range(levels):
        at = pl.ds(d * narrow, narrow)
        coarse_ref[at, :] = ctemp[at, :] + mrecv[:, d, :]


def joined_call(count, width, narrow, own, slab, operands):
    planes, rows, cf = own.shape
    _, crows, cc = slab.shape
    levels = crows // narrow
    f32, bf16 = jnp.float32, jnp.bfloat16
    vmem = pl.BlockSpec(memory_space=pltpu.VMEM)
    dma = pltpu.SemaphoreType.DMA
    return pl.pallas_call(
        functools.partial(joined, count, width, narrow),
        out_shape=(
            jax.ShapeDtypeStruct((planes, rows, cf), f32),
            jax.ShapeDtypeStruct((crows, cc), f32),
        ),
        in_specs=[pl.BlockSpec(memory_space=pl.ANY)] * 14,
        out_specs=(vmem,) * 2,
        scratch_shapes=[pltpu.VMEM(v.shape, f32) for v in (own, slab) + operands]
        + [
            dma((14,)),
            pltpu.VMEM((7, rows + 2 * width, 3 * cf), bf16),
            pltpu.VMEM((7, rows + 2 * width, 3 * cf), bf16),
            pltpu.VMEM((5, crows + 2 * narrow, 3 * cc), bf16),
            pltpu.VMEM((5, crows + 2 * narrow, 3 * cc), bf16),
            pltpu.VMEM((rows, cf), f32),
            pltpu.VMEM((crows, cc), f32),
            pltpu.VMEM((levels * width, 128), f32),
            pltpu.VMEM((9, 3 * cf, 2 * cf), bf16),
            pltpu.VMEM((9, 3 * cf, 2 * cf), bf16),
            pltpu.VMEM((9, 3 * cc, 2 * cc), bf16),
            pltpu.VMEM((9, 3 * cc, 2 * cc), bf16),
            pltpu.VMEM((9, 3 * cf, 2 * cc), bf16),
            pltpu.VMEM((rows, 2 * cf), f32),
            pltpu.VMEM((rows // 2, 2 * cf), f32),
            pltpu.VMEM((rows, 2 * cf), f32),
            pltpu.VMEM((rows, 2 * cf), f32),
            pltpu.VMEM((rows // 2, 2 * cf), f32),
            pltpu.VMEM((4, crows, cc), f32),
            pltpu.VMEM((count, levels, cf), f32),
            pltpu.VMEM((count, levels, cf), f32),
            pltpu.VMEM((count, levels, cc), f32),
            pltpu.VMEM((count, levels, cc), f32),
            pltpu.VMEM((rows, 128), f32),
            dma((7,)), dma((7,)),
            dma((count,)), dma((count,)), dma((count,)), dma((count,)),
        ],
        compiler_params=pltpu.CompilerParams(
            collective_id=0, has_side_effects=True, vmem_limit_bytes=60 * 2**20
        ),
        cost_estimate=pl.CostEstimate(flops=10**9, bytes_accessed=6 * 10**6, transcendentals=0),
    )(own, slab, *operands)


def split_weights(w):
    out, inner = w.shape[:2]
    moved = jnp.transpose(w, (2, 3, 4, 1, 0)).reshape(9, 3 * inner, out)
    high = lax.reduce_precision(moved, 8, 7)
    return jnp.concatenate([high, moved - high], axis=2).astype(jnp.bfloat16)


def shifted(value, steps):
    count = lax.axis_size("gx")
    pairs = [(i, i + steps) for i in range(count) if 0 <= i + steps < count]
    return lax.ppermute(value, "gx", pairs)


def per_device(
    fine_in, coarse_in,
    fine_wa, fine_ba, fine_wb, fine_bb,
    coarse_wa, coarse_ba, coarse_wb, coarse_bb,
    down_w, down_b, up_w, up_b,
):
    count = lax.axis_size("gx")
    cf, planes, depth, width = fine_in.shape
    cc, _, levels, narrow = coarse_in.shape
    own = jnp.transpose(fine_in, (1, 2, 3, 0)).reshape(planes, depth * width, cf)
    slab = jnp.transpose(coarse_in, (1, 2, 3, 0)).reshape(1, levels * narrow, cc)
    if depth * width <= ROWS:
        def taps(w, last):
            out, inner = w.shape[:2]
            if last == "in":
                return jnp.transpose(w, (2, 3, 4, 0, 1)).reshape(27, out, inner)
            return jnp.transpose(w, (2, 3, 4, 1, 0)).reshape(27, inner, out)

        fine_sum, coarse_sum = joined_call(
            count, width, narrow, own, slab,
            (
                taps(fine_wa, "in"), fine_ba[None], taps(fine_wb, "in"), fine_bb[None],
                taps(coarse_wa, "in"), coarse_ba[None], taps(coarse_wb, "in"), coarse_bb[None],
                taps(down_w, "out"), down_b[None], up_w, up_b[None],
            ),
        )
        fine_out = jax.nn.gelu(fine_sum.reshape(planes, depth, width, cf), approximate=False)
        coarse_out = jax.nn.gelu(coarse_sum.reshape(levels, narrow, cc), approximate=False)
        return (
            jnp.transpose(fine_out, (3, 0, 1, 2)),
            jnp.transpose(coarse_out, (2, 0, 1))[:, None],
        )
    f7 = jnp.concatenate(
        [shifted(own[1:], 2), shifted(own, 1), own, shifted(own, -1)], axis=0
    )
    c5 = jnp.concatenate(
        [shifted(slab, 2), shifted(slab, 1), slab, shifted(slab, -1), shifted(slab, -2)], axis=0
    )
    up = up_w.T
    up_high = lax.reduce_precision(up, 8, 7)
    wu = jnp.concatenate([up_high, up - up_high], axis=1).astype(jnp.bfloat16)
    frows, crows = depth * width, levels * narrow
    some = max(1, min(levels, ROWS // width))
    vmem = pl.BlockSpec(memory_space=pltpu.VMEM)
    large = frows > 1024
    stage = [pltpu.VMEM((frows, cf), jnp.float32), pltpu.SemaphoreType.DMA] if large else []
    fine, coarse, moved, projected = pl.pallas_call(
        functools.partial(compute, count, width, narrow),
        out_shape=(
            jax.ShapeDtypeStruct((planes, frows, cf), jnp.float32),
            jax.ShapeDtypeStruct((crows, cc), jnp.float32),
            jax.ShapeDtypeStruct((crows, cc), jnp.float32),
            jax.ShapeDtypeStruct((crows, cf), jnp.float32),
        ),
        in_specs=[pl.BlockSpec(memory_space=pl.ANY) if large else vmem] + [vmem] * 13,
        out_specs=(vmem,) * 4,
        scratch_shapes=[
            pltpu.VMEM((7, frows + 2 * width, 3 * cf), jnp.bfloat16),
            pltpu.VMEM((7, frows + 2 * width, 3 * cf), jnp.bfloat16),
            pltpu.VMEM((5, crows + 2 * narrow, 3 * cc), jnp.bfloat16),
            pltpu.VMEM((5, crows + 2 * narrow, 3 * cc), jnp.bfloat16),
            pltpu.VMEM((frows, cf), jnp.float32),
            pltpu.VMEM((crows, cc), jnp.float32),
            pltpu.VMEM((some * width, 128), jnp.float32),
        ] + stage,
        compiler_params=pltpu.CompilerParams(vmem_limit_bytes=(60 if large else 30) * 2**20),
        cost_estimate=pl.CostEstimate(flops=10**9, bytes_accessed=6 * 10**6, transcendentals=0),
    )(
        f7, c5,
        split_weights(fine_wa), fine_ba[None], split_weights(fine_wb), fine_bb[None],
        split_weights(coarse_wa), coarse_ba[None], split_weights(coarse_wb), coarse_bb[None],
        split_weights(down_w), down_b[None], wu, up_b[None],
    )
    both = jnp.concatenate(
        [
            jnp.transpose(moved.reshape(levels, narrow, cc), (1, 0, 2)),
            jnp.transpose(projected.reshape(levels, narrow, cf), (1, 0, 2)),
        ],
        axis=2,
    )
    arrived = lax.all_to_all(both, "gx", split_axis=0, concat_axis=0, tiled=True)
    reduced = jnp.transpose(arrived[:, :, :cc], (1, 0, 2))
    raised = jnp.transpose(arrived[:, :, cc:], (1, 0, 2))
    coarse_out = jax.nn.gelu(coarse.reshape(levels, narrow, cc) + reduced, approximate=False)
    raised = jnp.broadcast_to(
        raised[None, :, None, :, None, :], (planes, levels, depth // levels, narrow, width // narrow, cf)
    ).reshape(planes, depth, width, cf)
    fine_out = jax.nn.gelu(fine.reshape(planes, depth, width, cf) + raised, approximate=False)
    return (
        jnp.transpose(fine_out, (3, 0, 1, 2)),
        jnp.transpose(coarse_out, (2, 0, 1))[:, None],
    )


def solution(mesh):
    split = P(None, ("groups", "gx"), None, None)
    return jax.shard_map(
        per_device,
        mesh=mesh,
        in_specs=(split, split) + (P(),) * 12,
        out_specs=(split, split),
        check_vma=False,
    )
```
